32 devices in a mesh: rows: 2 (over y), mp: 16 (over z, x, core).
Axes of the slice: x: 2, y: 2, z: 4, core: 2. Of those that a mesh axis runs over, the one named last changes fastest.
Arguments:
- lam_out: bfloat16 [1024, 16, 1024], P('mp', 'rows'), may hold values from -6 to 6
- q_down: bfloat16 [1024, 4096], P(None, 'rows'), may hold values from -127 to 127, as said below
- down_scale: float32 [1024], replicated, may hold values from 0.0001 to 0.001
- q_up: bfloat16 [4096, 1024], P('rows'), may hold values from -127 to 127, as said below
- up_scale: float32 [4096], P('rows'), may hold values from 5e-05 to 0.0005
- chan_slopes: bfloat16 [2, 1024, 2, 4096], P(None, 'mp', 'rows'), may hold values from -0.14941406 to 1.09375
- chan_icpt: bfloat16 [2, 1024, 2, 4096], P(None, 'mp', 'rows')
- tok_in_blocks: bfloat16 [16, 128, 128], replicated, may hold values from -0.25 to 0.25
- tok_out_blocks: bfloat16 [16, 128, 128], replicated, may hold values from -0.25 to 0.25
- block_cells: int32 [16], replicated, may hold values from 0 to 31, as said below
- tok_slopes: bfloat16 [2, 512, 2, 1024], P(None, None, 'rows', 'mp'), may hold values from -0.14941406 to 1.09375
- tok_icpt: bfloat16 [2, 512, 2, 1024], P(None, None, 'rows', 'mp')
Outputs:
- lam_in: bfloat16 [1024, 16, 1024], P(None, 'rows', 'mp')
- bias: float32 [16], P('rows')
The draws below stay inside these ranges and needn't reach their ends.
Inputs may be any that keep to these rules, and one draw needn't show every extreme that they name: `q_down`: integer values, 8-bit signed codes; a program may carry them across devices in any exact packed form, several codes to an element. `q_up`: integer values, 8-bit signed codes; a program may carry them across devices in any exact packed form, several codes to an element. `block_cells`: 16 distinct cells; cell h * 8 + u is hidden block h and token block u.
All inputs are finite; a program needn't handle non-finite values.
Results may differ from the reference program's by a relative error of at most 0.012.
Values may be sent and summed in bfloat16 or wider, within the bound.
A program may use at most 128 MiB of HBM per device.

```python
import math
import jax
import jax.numpy as jnp
from jax import lax

D = 1024
CH = 4096
TH = 512
TOK = 1024
BLK = 128
NB = 16
SPEC = 8
IMAGES = 2
ROWS = 16
NHB = 4
NTB = 8


def draw_q_down(key, part):
    return jax.random.randint(jax.random.fold_in(key, 3), (D, CH), -127, 128).astype(jnp.bfloat16)


def draw_q_up(key, part):
    return jax.random.randint(jax.random.fold_in(key, 5), (CH, D), -127, 128).astype(jnp.bfloat16)


def draw_block_cells(key, part):
    return jax.random.permutation(jax.random.fold_in(key, 11), NHB * NTB)[:NB].astype(jnp.int32)


def draw_chan_icpt(key, part):
    inner = jax.random.fold_in(key, 7)
    noise = jax.random.normal(inner, (2, TOK, IMAGES, CH), jnp.float32)
    along_tok = 1.0 + 2.0 * jnp.arange(TOK, dtype=jnp.float32) / TOK
    along_hid = 1.0 + 2.0 * jnp.arange(CH, dtype=jnp.float32) / CH
    return (0.002 * noise * along_tok[None, :, None, None] * along_hid).astype(jnp.bfloat16)


def draw_tok_icpt(key, part):
    inner = jax.random.fold_in(key, 13)
    noise = jax.random.normal(inner, (2, TH, IMAGES, D), jnp.float32)
    along_chan = 1.0 + 2.0 * jnp.arange(D, dtype=jnp.float32) / D
    return (0.008 * noise * along_chan).astype(jnp.bfloat16)


def level_of(own_key, shape, pieces, least, largest):
    def one(axis_at, parts):
        draws = jax.random.uniform(jax.random.fold_in(jax.random.fold_in(own_key, 6), axis_at), (parts,), jnp.float32, least / len(pieces), largest / len(pieces))
        return jnp.repeat(jnp.exp(draws), shape[axis_at] // parts).reshape((-1,) + (1,) * (len(shape) - axis_at - 1))

    gain = one(*pieces[0])
    for cut in pieces[1:]:
        gain = gain * one(*cut)
    return gain


def normal_values(rng, extent, width, bound, pieces=(), kind=jnp.bfloat16):
    gain = level_of(rng, extent, pieces, -0.22, 0.18) if pieces else 1.0
    values = jax.random.normal(rng, extent, jnp.float32) * width * gain
    return jnp.minimum(jnp.maximum(values, -bound), bound).astype(kind)


def setup_inputs(seed: int = 0) -> dict:
    arg_keys = jax.random.split(jax.random.key(seed), 13)
    return {
        "lam_out": normal_values(arg_keys[0], (TOK, ROWS, D), 1.0, 6.0, ((0, 16), (1, 2))),
        "q_down": draw_q_down(jax.random.fold_in(arg_keys[12], 71), 0),
        "down_scale": jnp.clip(jnp.exp(jax.random.uniform(arg_keys[2], (D,), jnp.float32, math.log(0.0001), math.log(0.001))), 0.0001, 0.001),
        "q_up": draw_q_up(jax.random.fold_in(arg_keys[12], 71), 0),
        "up_scale": jnp.clip(jnp.exp(math.log(0.0005) - 2.3025852 * jax.random.uniform(arg_keys[4], (CH,), jnp.float32) ** level_of(arg_keys[4], (CH,), ((0, 2),), -0.2, 0.2)), 4.999999873689376e-05, 0.0005),
        "chan_slopes": jnp.clip(-0.14941406 + 1.2431641 * jax.random.uniform(arg_keys[5], (2, TOK, IMAGES, CH), jnp.float32) ** level_of(arg_keys[5], (2, TOK, IMAGES, CH), ((1, 16), (2, 2)), -0.2, 0.2), -0.14941406, 1.09375).astype(jnp.bfloat16),
        "chan_icpt": draw_chan_icpt(jax.random.fold_in(arg_keys[12], 71), 0),
        "tok_in_blocks": normal_values(arg_keys[7], (NB, BLK, BLK), (TOK // 2) ** -0.5, 0.25),
        "tok_out_blocks": normal_values(arg_keys[8], (NB, BLK, BLK), (TOK // 2) ** -0.5, 0.25),
        "block_cells": draw_block_cells(jax.random.fold_in(arg_keys[12], 71), 0),
        "tok_slopes": jnp.clip(-0.14941406 + 1.2431641 * jax.random.uniform(arg_keys[10], (2, TH, IMAGES, D), jnp.float32) ** level_of(arg_keys[10], (2, TH, IMAGES, D), ((2, 2), (3, 16)), -0.2, 0.2), -0.14941406, 1.09375).astype(jnp.bfloat16),
        "tok_icpt": draw_tok_icpt(jax.random.fold_in(arg_keys[12], 71), 0),
    }


def dense_blocks(blocks, cells, count_rows, count_cols):
    row_hot = (cells[:, None] // count_cols == jnp.arange(count_rows, dtype=jnp.int32)[None, :]).astype(jnp.float32)
    col_hot = (cells[:, None] % count_cols == jnp.arange(count_cols, dtype=jnp.int32)[None, :]).astype(jnp.float32)
    dense = jnp.einsum("bh,bt,bij->hitj", row_hot, col_hot, blocks.astype(jnp.float32))
    return dense.reshape(count_rows * BLK, count_cols * BLK).astype(jnp.bfloat16)


def reference(lam_out, q_down, down_scale, q_up, up_scale, chan_slopes, chan_icpt, tok_in_blocks, tok_out_blocks, block_cells, tok_slopes, tok_icpt):
    def channel_block(items):
        lam_blk, slope_blk, icpt_blk = items
        scaled = (lam_blk.astype(jnp.float32) * down_scale).astype(jnp.bfloat16)
        pre = jnp.dot(scaled.reshape(-1, D), q_down, preferred_element_type=jnp.float32)
        pre = pre.reshape(BLK, IMAGES, SPEC, CH)
        pos = jnp.maximum(pre, 0.0)
        neg = jnp.minimum(pre, 0.0)
        lower = slope_blk[0].astype(jnp.float32)[:, :, None, :]
        upper = slope_blk[1].astype(jnp.float32)[:, :, None, :]
        mid = pos * lower + neg * upper
        icpt_low = icpt_blk[0].astype(jnp.float32)[:, :, None, :]
        icpt_high = icpt_blk[1].astype(jnp.float32)[:, :, None, :]
        part_bias = jnp.sum(pos * icpt_low + neg * icpt_high, axis=(0, 3)).reshape(ROWS)
        mid_scaled = (mid * up_scale).astype(jnp.bfloat16).reshape(-1, CH)
        back = jnp.dot(mid_scaled, q_up, preferred_element_type=jnp.float32).reshape(BLK, ROWS, D)
        result = (lam_blk.astype(jnp.float32) + back).astype(jnp.bfloat16)
        return result, part_bias

    lam_blocks = lam_out.reshape(NTB, BLK, ROWS, D)
    slope_blocks = jnp.moveaxis(chan_slopes.reshape(2, NTB, BLK, IMAGES, CH), 1, 0)
    icpt_blocks = jnp.moveaxis(chan_icpt.reshape(2, NTB, BLK, IMAGES, CH), 1, 0)
    res_blocks, bias_parts = lax.map(channel_block, (lam_blocks, slope_blocks, icpt_blocks))
    lam_res = res_blocks.reshape(TOK, ROWS, D)
    bias_chan = jnp.sum(bias_parts, axis=0)

    tok_in = dense_blocks(tok_in_blocks, block_cells, NHB, NTB)
    swapped = (block_cells % NTB) * NHB + block_cells // NTB
    tok_out = dense_blocks(tok_out_blocks, swapped, NTB, NHB)
    columns = lam_res.reshape(TOK, ROWS * D)
    tpre = lax.dot_general(tok_out, columns, (((0,), (0,)), ((), ())), preferred_element_type=jnp.float32)
    tpre = tpre.reshape(TH, IMAGES, SPEC, D)
    pos = jnp.maximum(tpre, 0.0)
    neg = jnp.minimum(tpre, 0.0)
    lower = tok_slopes[0].astype(jnp.float32)[:, :, None, :]
    upper = tok_slopes[1].astype(jnp.float32)[:, :, None, :]
    tmid = (pos * lower + neg * upper).astype(jnp.bfloat16)
    icpt_low = tok_icpt[0].astype(jnp.float32)[:, :, None, :]
    icpt_high = tok_icpt[1].astype(jnp.float32)[:, :, None, :]
    bias_tok = jnp.sum(pos * icpt_low + neg * icpt_high, axis=(0, 3)).reshape(ROWS)
    back = lax.dot_general(tok_in, tmid.reshape(TH, ROWS * D), (((0,), (0,)), ((), ())), preferred_element_type=jnp.float32)
    lam_in = (lam_res.astype(jnp.float32) + back.reshape(TOK, ROWS, D)).astype(jnp.bfloat16)
    return lam_in, bias_chan + bias_tok
```

```python
import jax
import jax.numpy as jnp
from jax import lax
from jax.experimental import pallas as pl
from jax.experimental.pallas import tpu as pltpu
from jax.sharding import PartitionSpec as P

D = 1024
CH = 4096
TH = 512
TOK = 1024
BLK = 128
SPEC = 8
IMG_DEV = 1
NHB = 4
NTB = 8


def dense_blocks(blocks, cells, count_rows, count_cols):
    row_hot = (
        cells[:, None] // count_cols == jnp.arange(count_rows, dtype=jnp.int32)[None, :]
    ).astype(jnp.float32)
    col_hot = (
        cells[:, None] % count_cols == jnp.arange(count_cols, dtype=jnp.int32)[None, :]
    ).astype(jnp.float32)
    dense = jnp.einsum("bh,bt,bij->hitj", row_hot, col_hot, blocks.astype(jnp.float32))
    return dense.reshape(count_rows * BLK, count_cols * BLK).astype(jnp.bfloat16)


def relax(pre, slopes, icpt):
    pos = jnp.maximum(pre, 0.0)
    neg = jnp.minimum(pre, 0.0)
    lower = slopes[0].astype(jnp.float32)[:, :, None, :]
    upper = slopes[1].astype(jnp.float32)[:, :, None, :]
    icpt_low = icpt[0].astype(jnp.float32)[:, :, None, :]
    icpt_high = icpt[1].astype(jnp.float32)[:, :, None, :]
    mid = pos * lower + neg * upper
    row_bias = jnp.sum(pos * icpt_low + neg * icpt_high, axis=(0, 3)).reshape(-1)
    return (mid, row_bias)


def on_device(
    lam_out,
    q_down,
    down_scale,
    q_up,
    up_scale,
    chan_slopes,
    chan_icpt,
    tok_in_blocks,
    tok_out_blocks,
    block_cells,
    tok_slopes,
    tok_icpt,
):
    tok_dev = lam_out.shape[0]
    rows_dev = lam_out.shape[1]
    rows_all = rows_dev * lax.axis_size("rows")
    offset = lax.axis_index("rows") * rows_dev
    scaled = (lam_out.astype(jnp.float32) * down_scale).astype(jnp.bfloat16)
    flat = scaled.reshape(-1, D)
    pre = jnp.dot(
        flat, lax.all_gather(q_down, "rows", axis=1, tiled=True), preferred_element_type=jnp.float32
    )
    pre = pre.reshape(tok_dev, IMG_DEV, SPEC, CH)
    mid, own_bias = relax(pre, chan_slopes, chan_icpt)
    mid_flat = mid.reshape(-1, CH)
    codes = lax.all_gather(q_up, "rows", axis=0, tiled=True)
    scales = lax.all_gather(up_scale.astype(jnp.bfloat16), "rows", axis=0, tiled=True).astype(
        jnp.float32
    )
    weighted = (mid_flat * scales).astype(jnp.bfloat16)
    summed = jnp.dot(weighted, codes, preferred_element_type=jnp.float32)
    summed = summed.reshape(tok_dev, rows_dev, D)
    chan_bias = lax.dynamic_update_slice_in_dim(
        jnp.zeros((rows_all,), jnp.float32), own_bias, offset, 0
    )
    lam_res = (lam_out.astype(jnp.float32) + summed).astype(jnp.bfloat16)
    turned = lax.all_to_all(lam_res, "mp", split_axis=2, concat_axis=0, tiled=True)
    chan_dev = turned.shape[2]
    columns = turned.reshape(TOK, rows_dev * chan_dev)
    tok_in = dense_blocks(tok_in_blocks, block_cells, NHB, NTB)
    swapped = block_cells % NTB * NHB + block_cells // NTB
    tok_out = dense_blocks(tok_out_blocks, swapped, NTB, NHB)
    tpre = lax.dot_general(
        tok_out, columns, (((0,), (0,)), ((), ())), preferred_element_type=jnp.float32
    )
    tpre = tpre.reshape(TH, IMG_DEV, SPEC, chan_dev)
    tmid, tok_bias = relax(tpre, tok_slopes, tok_icpt)
    tmid = tmid.astype(jnp.bfloat16).reshape(TH, rows_dev * chan_dev)
    back = lax.dot_general(
        tok_in, tmid, (((0,), (0,)), ((), ())), preferred_element_type=jnp.float32
    )
    lam_in = (turned.astype(jnp.float32) + back.reshape(TOK, rows_dev, chan_dev)).astype(
        jnp.bfloat16
    )
    placed = lax.dynamic_update_slice_in_dim(
        jnp.zeros((rows_all,), jnp.float32), tok_bias, offset, 0
    )
    totals = lax.psum(chan_bias + placed, ("rows", "mp"))
    bias = lax.dynamic_slice_in_dim(totals, offset, rows_dev, 0)
    return (lam_in, bias)


MESH = pl.DeviceIdType.MESH
F32 = jnp.float32
BF16 = jnp.bfloat16
QW = 512
NP = 8
PR = 64


def fused_kernel(
    lam_hbm,
    qd_hbm,
    qu_hbm,
    ds_ref,
    us_ref,
    cs_hbm,
    ci_hbm,
    tin_hbm,
    tout_hbm,
    cells,
    ts_hbm,
    ti_hbm,
    out_ref,
    bias_ref,
    qd_v,
    qu_v,
    pk_qd,
    pk_qu,
    spk,
    pbuf,
    usr,
    cs_v,
    ci_v,
    lam_v,
    scaled,
    acc,
    wbuf,
    unp,
    bacc,
    sbuf,
    rb,
    xt,
    tin_v,
    tout_v,
    tin_d,
    tout_d,
    ts_v,
    ti_v,
    tmid,
    bsend,
    brecv,
    lsem,
    ssem,
    rsem,
    usem,
    a_s,
    a_r,
    b_s,
    b_r,
):
    y = lax.axis_index("rows")
    m = lax.axis_index("mp")
    q = lax.rem(m, 4)
    cb = lax.rem(m, 2)
    xb = lax.div(q, 2)
    xn = m + 2 - 4 * xb
    cn = m + 1 - 2 * cb
    qx = lax.rem(q + 2, 4)
    qc = q + 1 - 2 * cb
    qd = lax.rem(qc + 2, 4)
    half = QW * 4

    def local(src, dst, k):
        c = pltpu.make_async_copy(src, dst, lsem.at[k])
        c.start()
        return c

    c_pkd = local(qd_hbm.at[:, pl.ds(pl.multiple_of(q * QW, QW), QW)], pk_qd, 0)
    c_pku = local(qu_hbm.at[pl.ds(pl.multiple_of(q * QW, QW), QW), :], pk_qu, 1)
    c_lam = local(lam_hbm, lam_v, 2)
    loc = []
    for i in range(4):
        off = pl.multiple_of(y * half + i * QW, QW)
        loc.append(
            [
                local(qd_hbm.at[:, i * QW : (i + 1) * QW], qd_v.at[i], 3 + 4 * i),
                local(cs_hbm.at[:, :, pl.ds(off, QW)], cs_v.at[i], 4 + 4 * i),
                local(ci_hbm.at[:, :, pl.ds(off, QW)], ci_v.at[i], 5 + 4 * i),
                local(qu_hbm.at[i * QW : (i + 1) * QW, :], qu_v.at[i], 6 + 4 * i),
            ]
        )
    rem = []
    for i, qq in enumerate((q, qx, qc, qd)):
        off = pl.multiple_of((1 - y) * half + qq * QW, QW)
        rem.append(
            [
                local(cs_hbm.at[:, :, pl.ds(off, QW)], cs_v.at[4 + i], 19 + 2 * i),
                local(ci_hbm.at[:, :, pl.ds(off, QW)], ci_v.at[4 + i], 20 + 2 * i),
            ]
        )
    toks = [
        local(tin_hbm, tin_v, 27),
        local(tout_hbm, tout_v, 28),
        local(ts_hbm, ts_v, 29),
        local(ti_hbm, ti_v, 30),
    ]

    barrier = pltpu.get_barrier_semaphore()
    pl.semaphore_signal(barrier, inc=1, device_id=(1 - y, m), device_id_type=MESH)

    @pl.loop(1, 16)
    def _(k):
        pl.semaphore_signal(
            barrier, inc=1, device_id=(y, lax.rem(m + k, 16)), device_id_type=MESH
        )

    def pack(parts):
        w = None
        for k, part in enumerate(parts):
            code = part.astype(F32).astype(jnp.int32)
            code = (code & 255) << (8 * k) if k < 3 else code << 24
            w = code if w is None else w | code
        return w

    def y_copy(p):
        return pltpu.make_async_remote_copy(
            src_ref=spk.at[p],
            dst_ref=pbuf.at[q, p],
            send_sem=ssem.at[p],
            recv_sem=rsem.at[q, p],
            device_id=(1 - y, m),
            device_id_type=MESH,
        )

    def piece(slot, p, sem, dev):
        return pltpu.make_async_remote_copy(
            src_ref=pbuf.at[slot, p],
            dst_ref=pbuf.at[slot, p],
            send_sem=ssem.at[sem],
            recv_sem=rsem.at[slot, p],
            device_id=(y, dev),
            device_id_type=MESH,
        )

    def scale_copy():
        return pltpu.make_async_remote_copy(
            src_ref=us_ref,
            dst_ref=usr,
            send_sem=usem.at[0],
            recv_sem=usem.at[1],
            device_id=(1 - y, m),
            device_id_type=MESH,
        )

    c_pkd.wait()
    spk[0] = pack([pk_qd[i * 256 : i * 256 + PR, :] for i in range(4)])
    pl.semaphore_wait(barrier, 16)
    y_copy(0).start()
    for p in range(1, 4):
        spk[p] = pack([pk_qd[i * 256 + p * PR : i * 256 + (p + 1) * PR, :] for i in range(4)])
        y_copy(p).start()
    c_pku.wait()
    for p in range(4):
        spk[4 + p] = pack(
            [
                pk_qu[a * 256 + p * PR : a * 256 + (p + 1) * PR, b * QW : (b + 1) * QW]
                for a in range(2)
                for b in range(2)
            ]
        )
        y_copy(4 + p).start()
    scale_copy().start()

    c_lam.wait()
    flat = lam_v[...].astype(F32).reshape(512, D).astype(BF16)
    to = lax.broadcasted_iota(jnp.int32, (512, 512), 0)
    frm = lax.broadcasted_iota(jnp.int32, (512, 512), 1)
    perm = ((to & 63) * 8 + (to >> 6) == frm).astype(F32).astype(BF16)
    for n in range(2):
        cols = slice(n * 512, (n + 1) * 512)
        turned = jnp.dot(perm, flat[:, cols], preferred_element_type=F32)
        acc[:, cols] = turned
        scaled[:, cols] = (turned * ds_ref[:, cols]).astype(BF16)
    bacc[...] = jnp.zeros_like(bacc)

    def weights(codes, scale, s):
        @pl.loop(0, 2)
        def _(g):
            cols = pl.ds(pl.multiple_of(g * 256, 256), 256)
            pre = jnp.dot(scaled[...], codes[:, cols], preferred_element_type=F32)
            low = cs_v[s, 0, :, cols].astype(F32) * scale[:, cols]
            up = cs_v[s, 1, :, cols].astype(F32) * scale[:, cols]
            ilow = ci_v[s, 0, :, cols].astype(F32)
            iup = ci_v[s, 1, :, cols].astype(F32)
            for r in range(8):
                part = pre[r * 64 : (r + 1) * 64]
                pos = part > 0.0
                w = part * jnp.where(pos, low, up)
                wbuf[s, r * 64 : (r + 1) * 64, cols] = w.astype(BF16)
                b = (part * jnp.where(pos, ilow, iup)).reshape(8, 8, 256).sum(axis=0)
                bacc[r] = bacc[r] + (b[:, :128] + b[:, 128:])

    def add_back(codes, s):
        @pl.loop(0, 2)
        def _(g):
            cols = pl.ds(pl.multiple_of(g * 512, 512), 512)
            acc[:, cols] = acc[:, cols] + jnp.dot(
                wbuf[s], codes[:, cols], preferred_element_type=F32
            )

    def unpack(w, k):
        code = w << (24 - 8 * k) if k < 3 else w
        return (code >> 24).astype(F32).astype(BF16)

    def y_step(p):
        piece(q, p, 8, xn).wait_recv()
        piece(q, p, 8 + p, xn).start()
        piece(q, p, 16 + p, cn).start()

    def x_step(p):
        piece(qx, p, 8, cn).wait_recv()
        piece(qx, p, 24 + p, cn).start()

    def wait_pieces(slot, lo):
        for p in range(lo, lo + 4):
            piece(slot, p, 8, cn).wait_recv()

    def remote_weights(slot, i):
        for c in rem[i]:
            c.wait()
        for k in range(4):
            unp[k * 256 : (k + 1) * 256, :] = unpack(
                pbuf[slot, pl.ds(0, 4)].reshape(256, QW), k
            )
        weights(unp, usr.at[slot], 4 + i)

    def remote_codes(slot, i):
        w = pbuf[slot, pl.ds(4, 4)].reshape(256, QW)
        for k in range(4):
            a, b = k // 2, k % 2
            qu_v[i, a * 256 : (a + 1) * 256, b * QW : (b + 1) * QW] = unpack(w, k)

    def local_quarter(i):
        for c in loc[i]:
            c.wait()
        weights(qd_v.at[i], us_ref.at[i], i)
        add_back(qu_v.at[i], i)

    local_quarter(0)
    y_step(0)
    local_quarter(1)
    y_step(1)
    x_step(0)
    local_quarter(2)
    y_step(2)
    x_step(1)
    local_quarter(3)
    y_step(3)
    x_step(2)
    scale_copy().wait()
    remote_weights(q, 0)
    y_step(4)
    x_step(3)
    remote_weights(qx, 1)
    y_step(5)
    x_step(4)
    wait_pieces(qc, 0)
    remote_weights(qc, 2)
    y_step(6)
    x_step(5)
    wait_pieces(qd, 0)
    remote_weights(qd, 3)
    y_step(7)
    x_step(6)
    remote_codes(q, 0)
    add_back(qu_v.at[0], 4)
    x_step(7)
    remote_codes(qx, 1)
    wait_pieces(qc, 4)
    remote_codes(qc, 2)
    wait_pieces(qd, 4)
    remote_codes(qd, 3)

    def turn_copy(to_dev, src):
        return pltpu.make_async_remote_copy(
            src_ref=sbuf.at[to_dev],
            dst_ref=rb.at[:, pl.ds(pl.multiple_of(src * 64, 64), 64), :],
            send_sem=a_s.at[to_dev],
            recv_sem=a_r.at[src],
            device_id=(y, to_dev),
            device_id_type=MESH,
        )

    zb = lax.div(m, 4)
    order = (lax.rem(zb + 2, 4), 3 - zb, zb + 1 - 2 * lax.rem(zb, 2), zb)
    lane = lax.broadcasted_iota(jnp.int32, (256, 128), 1)
    for z in order:
        cols = pl.ds(pl.multiple_of(z * 256, 256), 256)
        total = acc[:, cols]
        for i in range(1, 4):
            total = total + jnp.dot(
                wbuf[4 + i], qu_v[i, :, cols], preferred_element_type=F32
            )
        for x in range(2):
            a = total[0:256, x * 128 : (x + 1) * 128]
            b = total[256:512, x * 128 : (x + 1) * 128]
            first = jnp.where(lane < 64, a, pltpu.roll(b, 64, 1))
            second = jnp.where(lane < 64, pltpu.roll(a, 64, 1), b)
            sbuf[z * 4 + 2 * x] = first.astype(BF16).reshape(4, 64, 128)
            sbuf[z * 4 + 2 * x + 1] = second.astype(BF16).reshape(4, 64, 128)
        if z is not zb:
            for k in range(4):
                turn_copy(z * 4 + k, m).start()
    xcn = xn + 1 - 2 * cb
    for dev in (xn, xcn, cn):
        turn_copy(dev, m).start()
    rb[:, pl.ds(pl.multiple_of(m * 64, 64), 64), :] = sbuf[m]

    for c in toks:
        c.wait()

    @pl.loop(0, NHB * NTB)
    def _(cell):
        at = jnp.int32(0)
        hits = jnp.int32(0)
        for b in range(16):
            hit = (cells[b] == cell).astype(jnp.int32)
            at = jnp.maximum(at, b * hit)
            hits = hits + hit
        on = hits.astype(F32)
        h = pl.multiple_of(lax.div(cell, NTB) * BLK, BLK)
        u = pl.multiple_of(lax.rem(cell, NTB) * BLK, BLK)
        tin_d[pl.ds(h, BLK), pl.ds(u, BLK)] = (tin_v[at].astype(F32) * on).astype(BF16)
        tout_d[pl.ds(u, BLK), pl.ds(h, BLK)] = (tout_v[at].astype(F32) * on).astype(BF16)

    def transpose_chip(chip):
        at = pl.ds(pl.multiple_of(chip * 128, 128), 128)
        for r in range(4):
            xt[r * 128 : (r + 1) * 128, at] = rb[r, at, :].astype(F32).T.astype(BF16)

    for z in order[:3]:
        for x in range(2):
            turn_copy(cn, z * 4 + 2 * x).wait_recv()
            turn_copy(cn, z * 4 + 2 * x + 1).wait_recv()
            transpose_chip(z * 2 + x)
    turn_copy(cn, xn).wait_recv()
    turn_copy(cn, xcn).wait_recv()
    transpose_chip(lax.div(xn, 2))
    turn_copy(cn, cn).wait_recv()
    transpose_chip(lax.div(m, 2))

    @pl.loop(0, 2)
    def _(g):
        rows = pl.ds(pl.multiple_of(g * 256, 256), 256)
        tpre = jnp.dot(xt[rows, :], tout_d[...], preferred_element_type=F32)
        low = ts_v[0].astype(F32)
        up = ts_v[1].astype(F32)
        ilow = ti_v[0].astype(F32)
        iup = ti_v[1].astype(F32)
        for j in range(4):
            part = tpre[j * 64 : (j + 1) * 64]
            pos = part > 0.0
            t = part * jnp.where(pos, low, up)
            tmid[pl.ds(pl.multiple_of(g * 256 + j * 64, 64), 64), :] = t.astype(BF16)
            b = (part * jnp.where(pos, ilow, iup)).reshape(8, 8, TH).sum(axis=0)
            b = b[:, :128] + b[:, 128:256] + b[:, 256:384] + b[:, 384:]
            r = g * 2 + j // 2 + 4 * (j % 2)
            bacc[r] = bacc[r] + b

    bsend[...] = jnp.sum(bacc[...], axis=1)

    def bias_copy(k, src):
        to_dev = lax.rem(m + k, 16)
        return pltpu.make_async_remote_copy(
            src_ref=bsend,
            dst_ref=brecv.at[src],
            send_sem=b_s.at[k],
            recv_sem=b_r.at[src],
            device_id=(y, to_dev),
            device_id_type=MESH,
        )

    @pl.loop(1, 16)
    def _(k):
        bias_copy(k, m).start()

    brecv[m] = bsend[...]

    for g in range(4):
        back = jnp.dot(
            tmid[g * 128 : (g + 1) * 128, :], tin_d[...], preferred_element_type=F32
        )
        total = (xt[g * 128 : (g + 1) * 128, :].astype(F32) + back).astype(BF16)
        out_ref[g] = total[:64]
        out_ref[g + 4] = total[64:]

    @pl.loop(1, 16)
    def _(k):
        bias_copy(k, lax.rem(m + 16 - k, 16)).wait_recv()

    total = jnp.sum(brecv[...], axis=0)
    bias_ref[...] = jnp.broadcast_to(jnp.sum(total, axis=1, keepdims=True), (8, 128))

    for p in range(NP):
        y_copy(p).wait_send()
        piece(q, p, 8 + p, xn).wait_send()
        piece(q, p, 16 + p, cn).wait_send()
        piece(qx, p, 24 + p, cn).wait_send()

    @pl.loop(1, 16)
    def _(k):
        turn_copy(lax.rem(m + k, 16), m).wait_send()
        bias_copy(k, m).wait_send()


def on_device_fused(
    lam_out,
    q_down,
    down_scale,
    q_up,
    up_scale,
    chan_slopes,
    chan_icpt,
    tok_in_blocks,
    tok_out_blocks,
    block_cells,
    tok_slopes,
    tok_icpt,
):
    hbm = pl.BlockSpec(memory_space=pl.ANY)
    vmem = pl.BlockSpec(memory_space=pltpu.VMEM)
    dma = pltpu.SemaphoreType.DMA
    ts = jnp.transpose(tok_slopes[:, :, 0, :], (0, 2, 1))
    ti = jnp.transpose(tok_icpt[:, :, 0, :], (0, 2, 1))
    out, bias = pl.pallas_call(
        fused_kernel,
        out_shape=(
            jax.ShapeDtypeStruct((8, 64, TOK), BF16),
            jax.ShapeDtypeStruct((8, 128), F32),
        ),
        in_specs=[
            hbm,
            hbm,
            hbm,
            vmem,
            vmem,
            hbm,
            hbm,
            hbm,
            hbm,
            pl.BlockSpec(memory_space=pltpu.SMEM),
            hbm,
            hbm,
        ],
        out_specs=(vmem, vmem),
        scratch_shapes=[
            pltpu.VMEM((4, D, QW), BF16),
            pltpu.VMEM((4, QW, D), BF16),
            pltpu.VMEM((D, QW), BF16),
            pltpu.VMEM((QW, D), BF16),
            pltpu.VMEM((NP, PR, QW), jnp.int32),
            pltpu.VMEM((4, NP, PR, QW), jnp.int32),
            pltpu.VMEM((4, 1, QW), F32),
            pltpu.VMEM((8, 2, 64, QW), BF16),
            pltpu.VMEM((8, 2, 64, QW), BF16),
            pltpu.VMEM((64, 8, D), BF16),
            pltpu.VMEM((512, D), BF16),
            pltpu.VMEM((512, D), F32),
            pltpu.VMEM((8, 512, QW), BF16),
            pltpu.VMEM((D, QW), BF16),
            pltpu.VMEM((8, 8, 128), F32),
            pltpu.VMEM((16, 4, 64, 128), BF16),
            pltpu.VMEM((4, TOK, 128), BF16),
            pltpu.VMEM((512, TOK), BF16),
            pltpu.VMEM((16, BLK, BLK), BF16),
            pltpu.VMEM((16, BLK, BLK), BF16),
            pltpu.VMEM((TH, TOK), BF16),
            pltpu.VMEM((TOK, TH), BF16),
            pltpu.VMEM((2, 64, TH), BF16),
            pltpu.VMEM((2, 64, TH), BF16),
            pltpu.VMEM((512, TH), BF16),
            pltpu.VMEM((8, 128), F32),
            pltpu.VMEM((16, 8, 128), F32),
            dma((31,)),
            dma((32,)),
            dma((4, NP)),
            dma((2,)),
            dma((16,)),
            dma((16,)),
            dma((16,)),
            dma((16,)),
        ],
        compiler_params=pltpu.CompilerParams(
            collective_id=0, has_side_effects=True, vmem_limit_bytes=56 * 1024 * 1024
        ),
    )(
        lam_out,
        q_down,
        q_up,
        down_scale.reshape(1, D),
        up_scale.reshape(4, 1, QW),
        chan_slopes[:, :, 0, :],
        chan_icpt[:, :, 0, :],
        tok_in_blocks,
        tok_out_blocks,
        block_cells,
        ts,
        ti,
    )
    return (jnp.transpose(out, (2, 0, 1)), bias[:, 0])


def solution(mesh):
    fits = mesh.shape['rows'] == 2 and mesh.shape['mp'] == 16
    return jax.shard_map(
        on_device_fused if fits else on_device,
        mesh=mesh,
        in_specs=(
            P("mp", "rows", None),
            P(None, "rows"),
            P(),
            P("rows", None),
            P("rows"),
            P(None, "mp", "rows", None),
            P(None, "mp", "rows", None),
            P(),
            P(),
            P(),
            P(None, None, "rows", "mp"),
            P(None, None, "rows", "mp"),
        ),
        out_specs=(P(None, "rows", "mp"), P("rows")),
        check_vma=False,
    )
```

```python
import jax
import jax.numpy as jnp
from jax import lax
from jax.experimental import pallas as pl
from jax.experimental.pallas import tpu as pltpu
from jax.sharding import PartitionSpec as P

D = 1024
CH = 4096
TH = 512
TOK = 1024
BLK = 128
SPEC = 8
IMG_DEV = 1
NHB = 4
NTB = 8


def dense_blocks(blocks, cells, count_rows, count_cols):
    row_hot = (
        cells[:, None] // count_cols == jnp.arange(count_rows, dtype=jnp.int32)[None, :]
    ).astype(jnp.float32)
    col_hot = (
        cells[:, None] % count_cols == jnp.arange(count_cols, dtype=jnp.int32)[None, :]
    ).astype(jnp.float32)
    dense = jnp.einsum("bh,bt,bij->hitj", row_hot, col_hot, blocks.astype(jnp.float32))
    return dense.reshape(count_rows * BLK, count_cols * BLK).astype(jnp.bfloat16)


def relax(pre, slopes, icpt):
    pos = jnp.maximum(pre, 0.0)
    neg = jnp.minimum(pre, 0.0)
    lower = slopes[0].astype(jnp.float32)[:, :, None, :]
    upper = slopes[1].astype(jnp.float32)[:, :, None, :]
    icpt_low = icpt[0].astype(jnp.float32)[:, :, None, :]
    icpt_high = icpt[1].astype(jnp.float32)[:, :, None, :]
    mid = pos * lower + neg * upper
    row_bias = jnp.sum(pos * icpt_low + neg * icpt_high, axis=(0, 3)).reshape(-1)
    return (mid, row_bias)


def on_device(
    lam_out,
    q_down,
    down_scale,
    q_up,
    up_scale,
    chan_slopes,
    chan_icpt,
    tok_in_blocks,
    tok_out_blocks,
    block_cells,
    tok_slopes,
    tok_icpt,
):
    tok_dev = lam_out.shape[0]
    rows_dev = lam_out.shape[1]
    rows_all = rows_dev * lax.axis_size("rows")
    offset = lax.axis_index("rows") * rows_dev
    scaled = (lam_out.astype(jnp.float32) * down_scale).astype(jnp.bfloat16)
    flat = scaled.reshape(-1, D)
    pre = jnp.dot(
        flat, lax.all_gather(q_down, "rows", axis=1, tiled=True), preferred_element_type=jnp.float32
    )
    pre = pre.reshape(tok_dev, IMG_DEV, SPEC, CH)
    mid, own_bias = relax(pre, chan_slopes, chan_icpt)
    mid_flat = mid.reshape(-1, CH)
    codes = lax.all_gather(q_up, "rows", axis=0, tiled=True)
    scales = lax.all_gather(up_scale.astype(jnp.bfloat16), "rows", axis=0, tiled=True).astype(
        jnp.float32
    )
    weighted = (mid_flat * scales).astype(jnp.bfloat16)
    summed = jnp.dot(weighted, codes, preferred_element_type=jnp.float32)
    summed = summed.reshape(tok_dev, rows_dev, D)
    chan_bias = lax.dynamic_update_slice_in_dim(
        jnp.zeros((rows_all,), jnp.float32), own_bias, offset, 0
    )
    lam_res = (lam_out.astype(jnp.float32) + summed).astype(jnp.bfloat16)
    turned = lax.all_to_all(lam_res, "mp", split_axis=2, concat_axis=0, tiled=True)
    chan_dev = turned.shape[2]
    columns = turned.reshape(TOK, rows_dev * chan_dev)
    tok_in = dense_blocks(tok_in_blocks, block_cells, NHB, NTB)
    swapped = block_cells % NTB * NHB + block_cells // NTB
    tok_out = dense_blocks(tok_out_blocks, swapped, NTB, NHB)
    tpre = lax.dot_general(
        tok_out, columns, (((0,), (0,)), ((), ())), preferred_element_type=jnp.float32
    )
    tpre = tpre.reshape(TH, IMG_DEV, SPEC, chan_dev)
    tmid, tok_bias = relax(tpre, tok_slopes, tok_icpt)
    tmid = tmid.astype(jnp.bfloat16).reshape(TH, rows_dev * chan_dev)
    back = lax.dot_general(
        tok_in, tmid, (((0,), (0,)), ((), ())), preferred_element_type=jnp.float32
    )
    lam_in = (turned.astype(jnp.float32) + back.reshape(TOK, rows_dev, chan_dev)).astype(
        jnp.bfloat16
    )
    placed = lax.dynamic_update_slice_in_dim(
        jnp.zeros((rows_all,), jnp.float32), tok_bias, offset, 0
    )
    totals = lax.psum(chan_bias + placed, ("rows", "mp"))
    bias = lax.dynamic_slice_in_dim(totals, offset, rows_dev, 0)
    return (lam_in, bias)


MESH = pl.DeviceIdType.MESH
F32 = jnp.float32
BF16 = jnp.bfloat16
QW = 512
EW = 256
NP = 4
PR = 128


def fused_kernel(
    lam_hbm,
    qd_hbm,
    qu_hbm,
    ds_ref,
    us_ref,
    us8_ref,
    cs_hbm,
    ci_hbm,
    tin_hbm,
    tout_hbm,
    cells,
    ts_hbm,
    ti_hbm,
    out_ref,
    bias_ref,
    qd_v,
    qu_v,
    pk_qd,
    pk_qu,
    spk,
    pbuf,
    usr,
    cs_v,
    ci_v,
    lam_v,
    scaled,
    acc,
    wbuf,
    unp,
    bacc,
    sbuf,
    rb,
    xt,
    tin_v,
    tout_v,
    tin_d,
    tout_d,
    ts_v,
    ti_v,
    tmid,
    bsend,
    brecv,
    lsem,
    ssem,
    rsem,
    usem,
    a_s,
    a_r,
    b_s,
    b_r,
):
    y = lax.axis_index("rows")
    m = lax.axis_index("mp")
    e = lax.rem(m, 8)
    cb = lax.rem(m, 2)
    xb = lax.rem(lax.div(m, 2), 2)
    zl = lax.div(e, 4)
    dx = 2 - 4 * xb
    dc = 1 - 2 * cb
    dz = 4 - 8 * zl
    xn = m + dx
    cn = m + dc
    zn = m + dz
    ex, ez, ed = e + dx, e + dz, e + dx + dz
    half = QW * 4

    def local(src, dst, k):
        c = pltpu.make_async_copy(src, dst, lsem.at[k])
        c.start()
        return c

    own = pl.multiple_of(e * EW, EW)
    c_pkd = local(qd_hbm.at[:, pl.ds(own, EW)], pk_qd, 0)
    c_pku = local(qu_hbm.at[pl.ds(own, EW), :], pk_qu, 1)
    c_lam = local(lam_hbm, lam_v, 2)
    loc = []
    for i in range(4):
        off = pl.multiple_of(y * half + i * QW, QW)
        loc.append(
            [
                local(qd_hbm.at[:, i * QW : (i + 1) * QW], qd_v.at[i], 3 + 4 * i),
                local(cs_hbm.at[:, :, pl.ds(off, QW)], cs_v.at[i], 4 + 4 * i),
                local(ci_hbm.at[:, :, pl.ds(off, QW)], ci_v.at[i], 5 + 4 * i),
                local(qu_hbm.at[i * QW : (i + 1) * QW, :], qu_v.at[i], 6 + 4 * i),
            ]
        )
    rem = []
    for i, base in enumerate((e, ex, ez, ed)):
        for h in range(2):
            off = pl.multiple_of((1 - y) * half + (base + h * dc) * EW, EW)
            dst = pl.ds(h * EW, EW)
            k = 19 + 4 * i + 2 * h
            rem.append(
                [
                    local(cs_hbm.at[:, :, pl.ds(off, EW)], cs_v.at[4 + i, :, :, dst], k),
                    local(ci_hbm.at[:, :, pl.ds(off, EW)], ci_v.at[4 + i, :, :, dst], k + 1),
                ]
            )
    toks = [
        local(tin_hbm, tin_v, 35),
        local(tout_hbm, tout_v, 36),
        local(ts_hbm, ts_v, 37),
        local(ti_hbm, ti_v, 38),
    ]

    barrier = pltpu.get_barrier_semaphore()
    pl.semaphore_signal(barrier, inc=1, device_id=(1 - y, m), device_id_type=MESH)

    @pl.loop(1, 16)
    def _(k):
        pl.semaphore_signal(
            barrier, inc=1, device_id=(y, lax.rem(m + k, 16)), device_id_type=MESH
        )

    def pack(parts):
        w = None
        for k, part in enumerate(parts):
            code = part.astype(F32).astype(jnp.int32)
            code = (code & 255) << (8 * k) if k < 3 else code << 24
            w = code if w is None else w | code
        return w

    def y_copy(p):
        return pltpu.make_async_remote_copy(
            src_ref=spk.at[p],
            dst_ref=pbuf.at[e, p],
            send_sem=ssem.at[p],
            recv_sem=rsem.at[e, p],
            device_id=(1 - y, m),
            device_id_type=MESH,
        )

    def piece(slot, p, sem, dev):
        return pltpu.make_async_remote_copy(
            src_ref=pbuf.at[slot, p],
            dst_ref=pbuf.at[slot, p],
            send_sem=ssem.at[sem],
            recv_sem=rsem.at[slot, p],
            device_id=(y, dev),
            device_id_type=MESH,
        )

    def scale_copy():
        return pltpu.make_async_remote_copy(
            src_ref=us8_ref,
            dst_ref=usr,
            send_sem=usem.at[0],
            recv_sem=usem.at[1],
            device_id=(1 - y, m),
            device_id_type=MESH,
        )

    c_pkd.wait()
    spk[0] = pack([pk_qd[i * 256 : i * 256 + PR, :] for i in range(4)])
    pl.semaphore_wait(barrier, 16)
    y_copy(0).start()
    spk[1] = pack([pk_qd[i * 256 + PR : i * 256 + 2 * PR, :] for i in range(4)])
    y_copy(1).start()
    c_pku.wait()
    for p in range(2):
        spk[2 + p] = pack(
            [pk_qu[p * PR : (p + 1) * PR, b * 256 : (b + 1) * 256] for b in range(4)]
        )
        y_copy(2 + p).start()
    scale_copy().start()

    c_lam.wait()
    flat = lam_v[...].astype(F32).reshape(512, D).astype(BF16)
    to = lax.broadcasted_iota(jnp.int32, (512, 512), 0)
    frm = lax.broadcasted_iota(jnp.int32, (512, 512), 1)
    perm = ((to & 63) * 8 + (to >> 6) == frm).astype(F32).astype(BF16)
    for n in range(2):
        cols = slice(n * 512, (n + 1) * 512)
        turned = jnp.dot(perm, flat[:, cols], preferred_element_type=F32)
        acc[:, cols] = turned
        scaled[:, cols] = (turned * ds_ref[:, cols]).astype(BF16)
    bacc[...] = jnp.zeros_like(bacc)

    def weights(codes, scale, s, cols):
        pre = jnp.dot(scaled[...], codes, preferred_element_type=F32)
        low = cs_v[s, 0, :, cols].astype(F32) * scale
        up = cs_v[s, 1, :, cols].astype(F32) * scale
        ilow = ci_v[s, 0, :, cols].astype(F32)
        iup = ci_v[s, 1, :, cols].astype(F32)
        for r in range(8):
            part = pre[r * 64 : (r + 1) * 64]
            pos = part > 0.0
            w = part * jnp.where(pos, low, up)
            wbuf[s, r * 64 : (r + 1) * 64, cols] = w.astype(BF16)
            b = (part * jnp.where(pos, ilow, iup)).reshape(8, 8, 256).sum(axis=0)
            bacc[r] = bacc[r] + (b[:, :128] + b[:, 128:])

    def add_back(codes, s):
        @pl.loop(0, 2)
        def _(g):
            cols = pl.ds(pl.multiple_of(g * 512, 512), 512)
            acc[:, cols] = acc[:, cols] + jnp.dot(
                wbuf[s], codes[:, cols], preferred_element_type=F32
            )

    def unpack(w, k):
        code = w << (24 - 8 * k) if k < 3 else w
        return (code >> 24).astype(F32).astype(BF16)

    def y_step(p):
        piece(e, p, 4, xn).wait_recv()
        piece(e, p, 4 + p, xn).start()
        piece(e, p, 8 + p, zn).start()
        piece(e, p, 12 + p, cn).start()

    def x_step(p):
        piece(ex, p, 4, cn).wait_recv()
        if p % 2 == 0:
            piece(ex, p, 28 + p, zn).start()
        piece(ex, p, 16 + p, cn).start()

    def z_step(p):
        piece(ez, p, 4, cn).wait_recv()
        if p % 2 == 1:
            piece(ez, p, 28 + p, xn).start()
        piece(ez, p, 20 + p, cn).start()

    def d_step(p):
        piece(ed, p, 4, cn).wait_recv()
        piece(ed, p, 24 + p, cn).start()

    def wait_core(slot, lo):
        for p in range(lo, lo + 2):
            piece(slot + dc, p, 4, cn).wait_recv()

    def remote_weights(slot, i, h):
        if h:
            wait_core(slot, 0)
            slot = slot + dc
        for c in rem[2 * i + h]:
            c.wait()
        w = pbuf[slot, pl.ds(0, 2)].reshape(256, EW)
        for k in range(4):
            unp[k * 256 : (k + 1) * 256, :] = unpack(w, k)
        weights(unp[...], usr[slot], 4 + i, pl.ds(h * EW, EW))

    def remote_codes(slot, i, h):
        if h:
            wait_core(slot, 2)
            slot = slot + dc
        w = pbuf[slot, pl.ds(2, 2)].reshape(256, EW)
        for k in range(4):
            qu_v[i, h * EW : (h + 1) * EW, k * 256 : (k + 1) * 256] = unpack(w, k)

    def local_quarter(i):
        for c in loc[i]:
            c.wait()

        @pl.loop(0, 2)
        def _(g):
            cols = pl.ds(pl.multiple_of(g * 256, 256), 256)
            weights(qd_v[i, :, cols], us_ref[i, :, cols], i, cols)

        add_back(qu_v.at[i], i)

    local_quarter(0)
    y_step(0)
    local_quarter(1)
    y_step(1)
    x_step(0)
    z_step(0)
    local_quarter(2)
    y_step(2)
    x_step(1)
    z_step(1)
    scale_copy().wait()
    remote_weights(e, 0, 0)
    remote_weights(ex, 1, 0)
    y_step(3)
    d_step(0)
    d_step(1)
    local_quarter(3)
    remote_weights(ez, 2, 0)
    x_step(2)
    z_step(2)
    remote_weights(e, 0, 1)
    remote_weights(ed, 3, 0)
    x_step(3)
    z_step(3)
    remote_weights(ex, 1, 1)
    remote_weights(ez, 2, 1)
    remote_weights(ed, 3, 1)
    remote_codes(e, 0, 0)
    remote_codes(e, 0, 1)
    d_step(2)
    d_step(3)
    add_back(qu_v.at[0], 4)
    for h in range(2):
        remote_codes(ex, 1, h)
        remote_codes(ez, 2, h)
        remote_codes(ed, 3, h)

    def turn_copy(to_dev, src):
        return pltpu.make_async_remote_copy(
            src_ref=sbuf.at[to_dev],
            dst_ref=rb.at[:, pl.ds(pl.multiple_of(src * 64, 64), 64), :],
            send_sem=a_s.at[to_dev],
            recv_sem=a_r.at[src],
            device_id=(y, to_dev),
            device_id_type=MESH,
        )

    zb = lax.div(m, 4)
    order = (lax.rem(zb + 2, 4), zb + 1 - 2 * lax.rem(zb, 2), 3 - zb, zb)
    lane = lax.broadcasted_iota(jnp.int32, (256, 128), 1)
    for z in order:
        cols = pl.ds(pl.multiple_of(z * 256, 256), 256)
        total = acc[:, cols]
        for i in range(1, 4):
            total = total + jnp.dot(
                wbuf[4 + i], qu_v[i, :, cols], preferred_element_type=F32
            )
        for x in range(2):
            a = total[0:256, x * 128 : (x + 1) * 128]
            b = total[256:512, x * 128 : (x + 1) * 128]
            first = jnp.where(lane < 64, a, pltpu.roll(b, 64, 1))
            second = jnp.where(lane < 64, pltpu.roll(a, 64, 1), b)
            sbuf[z * 4 + 2 * x] = first.astype(BF16).reshape(4, 64, 128)
            sbuf[z * 4 + 2 * x + 1] = second.astype(BF16).reshape(4, 64, 128)
        if z is not zb:
            for k in range(4):
                turn_copy(z * 4 + k, m).start()
    xcn = xn + 1 - 2 * cb
    for dev in (xn, xcn, cn):
        turn_copy(dev, m).start()
    rb[:, pl.ds(pl.multiple_of(m * 64, 64), 64), :] = sbuf[m]

    for c in toks:
        c.wait()

    @pl.loop(0, NHB * NTB)
    def _(cell):
        at = jnp.int32(0)
        hits = jnp.int32(0)
        for b in range(16):
            hit = (cells[b] == cell).astype(jnp.int32)
            at = jnp.maximum(at, b * hit)
            hits = hits + hit
        on = hits.astype(F32)
        h = pl.multiple_of(lax.div(cell, NTB) * BLK, BLK)
        u = pl.multiple_of(lax.rem(cell, NTB) * BLK, BLK)
        tin_d[pl.ds(h, BLK), pl.ds(u, BLK)] = (tin_v[at].astype(F32) * on).astype(BF16)
        tout_d[pl.ds(u, BLK), pl.ds(h, BLK)] = (tout_v[at].astype(F32) * on).astype(BF16)

    def transpose_chip(chip):
        at = pl.ds(pl.multiple_of(chip * 128, 128), 128)
        for r in range(4):
            xt[r * 128 : (r + 1) * 128, at] = rb[r, at, :].astype(F32).T.astype(BF16)

    for z in order[:3]:
        for x in range(2):
            turn_copy(cn, z * 4 + 2 * x).wait_recv()
            turn_copy(cn, z * 4 + 2 * x + 1).wait_recv()
            transpose_chip(z * 2 + x)
    turn_copy(cn, xn).wait_recv()
    turn_copy(cn, xcn).wait_recv()
    transpose_chip(lax.div(xn, 2))
    turn_copy(cn, cn).wait_recv()
    transpose_chip(lax.div(m, 2))

    @pl.loop(0, 2)
    def _(g):
        rows = pl.ds(pl.multiple_of(g * 256, 256), 256)
        tpre = jnp.dot(xt[rows, :], tout_d[...], preferred_element_type=F32)
        low = ts_v[0].astype(F32)
        up = ts_v[1].astype(F32)
        ilow = ti_v[0].astype(F32)
        iup = ti_v[1].astype(F32)
        for j in range(4):
            part = tpre[j * 64 : (j + 1) * 64]
            pos = part > 0.0
            t = part * jnp.where(pos, low, up)
            tmid[pl.ds(pl.multiple_of(g * 256 + j * 64, 64), 64), :] = t.astype(BF16)
            b = (part * jnp.where(pos, ilow, iup)).reshape(8, 8, TH).sum(axis=0)
            b = b[:, :128] + b[:, 128:256] + b[:, 256:384] + b[:, 384:]
            r = g * 2 + j // 2 + 4 * (j % 2)
            bacc[r] = bacc[r] + b

    bsend[...] = jnp.sum(bacc[...], axis=1)

    def bias_copy(k, src):
        to_dev = lax.rem(m + k, 16)
        return pltpu.make_async_remote_copy(
            src_ref=bsend,
            dst_ref=brecv.at[src],
            send_sem=b_s.at[k],
            recv_sem=b_r.at[src],
            device_id=(y, to_dev),
            device_id_type=MESH,
        )

    @pl.loop(1, 16)
    def _(k):
        bias_copy(k, m).start()

    brecv[m] = bsend[...]

    for g in range(4):
        back = jnp.dot(
            tmid[g * 128 : (g + 1) * 128, :], tin_d[...], preferred_element_type=F32
        )
        total = (xt[g * 128 : (g + 1) * 128, :].astype(F32) + back).astype(BF16)
        out_ref[g] = total[:64]
        out_ref[g + 4] = total[64:]

    @pl.loop(1, 16)
    def _(k):
        bias_copy(k, lax.rem(m + 16 - k, 16)).wait_recv()

    total = jnp.sum(brecv[...], axis=0)
    bias_ref[...] = jnp.broadcast_to(jnp.sum(total, axis=1, keepdims=True), (8, 128))

    for p in range(NP):
        y_copy(p).wait_send()
        piece(e, p, 4 + p, xn).wait_send()
        piece(e, p, 8 + p, zn).wait_send()
        piece(e, p, 12 + p, cn).wait_send()
        piece(ex, p, 16 + p, cn).wait_send()
        piece(ez, p, 20 + p, cn).wait_send()
        piece(ed, p, 24 + p, cn).wait_send()
        if p % 2 == 0:
            piece(ex, p, 28 + p, zn).wait_send()
        else:
            piece(ez, p, 28 + p, xn).wait_send()

    @pl.loop(1, 16)
    def _(k):
        turn_copy(lax.rem(m + k, 16), m).wait_send()
        bias_copy(k, m).wait_send()


def on_device_fused(
    lam_out,
    q_down,
    down_scale,
    q_up,
    up_scale,
    chan_slopes,
    chan_icpt,
    tok_in_blocks,
    tok_out_blocks,
    block_cells,
    tok_slopes,
    tok_icpt,
):
    hbm = pl.BlockSpec(memory_space=pl.ANY)
    vmem = pl.BlockSpec(memory_space=pltpu.VMEM)
    dma = pltpu.SemaphoreType.DMA
    ts = jnp.transpose(tok_slopes[:, :, 0, :], (0, 2, 1))
    ti = jnp.transpose(tok_icpt[:, :, 0, :], (0, 2, 1))
    out, bias = pl.pallas_call(
        fused_kernel,
        out_shape=(
            jax.ShapeDtypeStruct((8, 64, TOK), BF16),
            jax.ShapeDtypeStruct((8, 128), F32),
        ),
        in_specs=[
            hbm,
            hbm,
            hbm,
            vmem,
            vmem,
            vmem,
            hbm,
            hbm,
            hbm,
            hbm,
            pl.BlockSpec(memory_space=pltpu.SMEM),
            hbm,
            hbm,
        ],
        out_specs=(vmem, vmem),
        scratch_shapes=[
            pltpu.VMEM((4, D, QW), BF16),
            pltpu.VMEM((4, QW, D), BF16),
            pltpu.VMEM((D, EW), BF16),
            pltpu.VMEM((EW, D), BF16),
            pltpu.VMEM((NP, PR, EW), jnp.int32),
            pltpu.VMEM((8, NP, PR, EW), jnp.int32),
            pltpu.VMEM((8, 1, EW), F32),
            pltpu.VMEM((8, 2, 64, QW), BF16),
            pltpu.VMEM((8, 2, 64, QW), BF16),
            pltpu.VMEM((64, 8, D), BF16),
            pltpu.VMEM((512, D), BF16),
            pltpu.VMEM((512, D), F32),
            pltpu.VMEM((8, 512, QW), BF16),
            pltpu.VMEM((D, EW), BF16),
            pltpu.VMEM((8, 8, 128), F32),
            pltpu.VMEM((16, 4, 64, 128), BF16),
            pltpu.VMEM((4, TOK, 128), BF16),
            pltpu.VMEM((512, TOK), BF16),
            pltpu.VMEM((16, BLK, BLK), BF16),
            pltpu.VMEM((16, BLK, BLK), BF16),
            pltpu.VMEM((TH, TOK), BF16),
            pltpu.VMEM((TOK, TH), BF16),
            pltpu.VMEM((2, 64, TH), BF16),
            pltpu.VMEM((2, 64, TH), BF16),
            pltpu.VMEM((512, TH), BF16),
            pltpu.VMEM((8, 128), F32),
            pltpu.VMEM((16, 8, 128), F32),
            dma((39,)),
            dma((32,)),
            dma((8, NP)),
            dma((2,)),
            dma((16,)),
            dma((16,)),
            dma((16,)),
            dma((16,)),
        ],
        compiler_params=pltpu.CompilerParams(
            collective_id=0, has_side_effects=True, vmem_limit_bytes=56 * 1024 * 1024
        ),
    )(
        lam_out,
        q_down,
        q_up,
        down_scale.reshape(1, D),
        up_scale.reshape(4, 1, QW),
        up_scale.reshape(8, 1, EW),
        chan_slopes[:, :, 0, :],
        chan_icpt[:, :, 0, :],
        tok_in_blocks,
        tok_out_blocks,
        block_cells,
        ts,
        ti,
    )
    return (jnp.transpose(out, (2, 0, 1)), bias[:, 0])


def solution(mesh):
    fits = mesh.shape['rows'] == 2 and mesh.shape['mp'] == 16
    return jax.shard_map(
        on_device_fused if fits else on_device,
        mesh=mesh,
        in_specs=(
            P("mp", "rows", None),
            P(None, "rows"),
            P(),
            P("rows", None),
            P("rows"),
            P(None, "mp", "rows", None),
            P(None, "mp", "rows", None),
            P(),
            P(),
            P(),
            P(None, None, "rows", "mp"),
            P(None, None, "rows", "mp"),
        ),
        out_specs=(P(None, "rows", "mp"), P("rows")),
        check_vma=False,
    )
```
